256 devices in a mesh: tm: 128 (over y, x_lo, z, core), mp: 2 (over x_hi).
Axes of the slice: x: 4 (x_hi: 2, x_lo: 2; x = x_hi * 2 + x_lo), y: 4, z: 8, core: 2. Of those that a mesh axis runs over, the one named last changes fastest.
Arguments:
- global_q: bfloat16 [4096, 2048], P('tm', 'mp'), may hold values from -9 to 9
- global_k: bfloat16 [4096, 2048], P('tm', 'mp'), may hold values from -7 to 7
- global_v: bfloat16 [4096, 2048], P('tm', 'mp'), may hold values from -6 to 6
- keyframe_mask: int32 [128], P('tm'), may hold values 0 or 1
- global_wo: bfloat16 [2048, 2048], P('mp'), may hold values from -0.125 to 0.125
- local_q: bfloat16 [123904, 2048], P('tm', 'mp'), may hold values from -9 to 9, as said below
- local_k: bfloat16 [123904, 2048], P('tm', 'mp'), may hold values from -7 to 7, as said below
- local_v: bfloat16 [123904, 2048], P('tm', 'mp'), may hold values from -6 to 6
- anchor_k: bfloat16 [11264, 2048], P('tm', 'mp'), may hold values from -7 to 7
- anchor_v: bfloat16 [11264, 2048], P('tm', 'mp'), may hold values from -6 to 6
Outputs:
- global_out: bfloat16 [4096, 2048], P('tm', 'mp')
- local_out: bfloat16 [123904, 2048], P('tm', 'mp')
The draws below stay inside these ranges and needn't reach their ends.
Inputs may be any that keep to these rules, and one draw needn't show every extreme that they name: `local_q`: entries of the generated frames' queries. `local_k`: entries of the generated frames' keys.
All inputs are finite; a program needn't handle non-finite values. No bound on the sum of `keyframe_mask` on one device may be relied on, other than what follows from the above.
Results may differ from the reference program's by a relative error of at most 0.014.
Values may be sent and summed in bfloat16 or wider, within the bound.
A program may use at most 128 MiB of HBM per device.

```python
import jax
import jax.numpy as jnp
from jax import lax

D = 2048
HEADS = 16
HD = 128
INFILL = 11
PG = 32
PL = 88
KEYFRAMES = 128
KEYS_G = 4096
LOCAL_ROWS = 123904


def spread_rows(key, rows, cols, scale):
    values = jax.random.normal(key, (rows, cols), jnp.float32) * scale
    return jnp.clip(values, -3.0 * scale, 3.0 * scale)


def draw_global_q(key, part):
    key = jax.random.fold_in(key, 11)
    return spread_rows(key, KEYS_G, HEADS * HD, 3.0).astype(jnp.bfloat16)


def draw_global_k(key, part):
    key = jax.random.fold_in(key, 12)
    return spread_rows(key, KEYS_G, HEADS * HD, 1.0).astype(jnp.bfloat16)


def draw_local_q(key, part):
    key = jax.random.fold_in(key, 13)
    return spread_rows(key, LOCAL_ROWS, HEADS * HD, 3.0).astype(jnp.bfloat16)


def draw_local_k(key, part):
    key = jax.random.fold_in(key, 14)
    return spread_rows(key, LOCAL_ROWS, HEADS * HD, 1.0).astype(jnp.bfloat16)


def draw_anchor_k(key, part):
    key = jax.random.fold_in(key, 15)
    return spread_rows(key, KEYFRAMES * PL, HEADS * HD, 1.0).astype(jnp.bfloat16)


def with_ends(array, stream_key, low, largest):
    longest = array.shape.index(max(array.shape))
    spots = []
    for shift in (0, 1):
        where = [jax.random.randint(jax.random.fold_in(stream_key, axis), (), 0, length) for axis, length in enumerate(array.shape)]
        where[longest] = (where[longest] + shift) % array.shape[longest]
        spots.append(tuple(where))
    return array.at[spots[0]].set(low).at[spots[1]].set(largest)


def level_of(own_key, shape, cuts, low, high):
    loudness, own = 1.0, jax.random.fold_in(own_key, 6)
    for axis_at, parts in cuts:
        draws = jnp.exp(jax.random.uniform(jax.random.fold_in(own, axis_at), (parts,), jnp.float32, low / len(cuts), high / len(cuts)))
        loudness = loudness * jnp.repeat(draws, shape[axis_at] // parts).reshape([-1 if axis == axis_at else 1 for axis in range(len(shape))])
    return loudness


def noise(own_key, dims, scale, most, cuts=(), kind=jnp.bfloat16):
    entries = jax.random.normal(own_key, dims, jnp.float32) * scale
    if len(cuts) > 0:
        entries = level_of(own_key, dims, cuts, -0.22, 0.18) * entries
    return jnp.clip(entries, min=-most, max=most).astype(kind)


def setup_inputs(seed: int = 0) -> dict:
    arg_keys = jax.random.split(jax.random.key(seed), 11)
    return {
        "global_q": draw_global_q(jax.random.fold_in(arg_keys[10], 71), 0),
        "global_k": draw_global_k(jax.random.fold_in(arg_keys[10], 71), 0),
        "global_v": noise(arg_keys[2], (KEYS_G, HEADS * HD), 1.0, 6.0, ((0, 128), (1, 2))),
        "keyframe_mask": with_ends((jax.random.randint(arg_keys[3], (KEYFRAMES,), 0, 4) < 1).astype(jnp.int32), jax.random.fold_in(arg_keys[3], 1), 0, 1),
        "global_wo": noise(arg_keys[4], (HEADS * HD, D), (HEADS * HD) ** -0.5, 0.125, ((0, 2),)),
        "local_q": draw_local_q(jax.random.fold_in(arg_keys[10], 71), 0),
        "local_k": draw_local_k(jax.random.fold_in(arg_keys[10], 71), 0),
        "local_v": noise(arg_keys[7], (LOCAL_ROWS, HEADS * HD), 1.0, 6.0, ((0, 128), (1, 2))),
        "anchor_k": draw_anchor_k(jax.random.fold_in(arg_keys[10], 71), 0),
        "anchor_v": noise(arg_keys[9], (KEYFRAMES * PL, HEADS * HD), 1.0, 6.0, ((0, 128), (1, 2))),
    }


def head_split(rows):
    return jnp.transpose(rows.astype(jnp.float32).reshape(rows.shape[0], HEADS, HD), (1, 0, 2))


def head_raw(rows):
    return jnp.transpose(rows.reshape(rows.shape[0], HEADS, HD), (1, 0, 2))


def reference(global_q, global_k, global_v, keyframe_mask, global_wo, local_q, local_k, local_v, anchor_k, anchor_v):
    factor = 1.0 / (HD ** 0.5)
    frame_given = jnp.repeat(keyframe_mask, PG)
    allowed = (frame_given[:, None] == 0) | (frame_given[None, :] == 1)

    def global_head(operands):
        q_one, k_one, v_one = operands
        scores = jnp.dot(q_one, k_one.T, precision=lax.Precision.HIGHEST) * factor
        scores = jnp.where(allowed, scores, -1e30)
        peak = jnp.max(scores, axis=1, keepdims=True)
        weights = jnp.where(allowed, jnp.exp(scores - peak), 0.0)
        total = jnp.sum(weights, axis=1, keepdims=True)
        rounded = weights.astype(jnp.bfloat16)
        return jnp.dot(rounded, v_one, preferred_element_type=jnp.float32) / total

    attended = lax.map(global_head, (head_split(global_q), head_split(global_k), head_raw(global_v)))
    attended = jnp.transpose(attended, (1, 0, 2)).reshape(KEYS_G, HEADS * HD).astype(jnp.bfloat16)
    global_out = jnp.dot(attended, global_wo, preferred_element_type=jnp.float32).astype(jnp.bfloat16)

    seg_rows = INFILL * PL
    q_seg = local_q.reshape(KEYFRAMES, seg_rows, HEADS * HD)
    k_seg = local_k.reshape(KEYFRAMES, seg_rows, HEADS * HD)
    v_seg = local_v.reshape(KEYFRAMES, seg_rows, HEADS * HD)
    a_k = anchor_k.reshape(KEYFRAMES, PL, HEADS * HD)
    a_v = anchor_v.reshape(KEYFRAMES, PL, HEADS * HD)
    r_k = jnp.roll(a_k, -1, axis=0)
    r_v = jnp.roll(a_v, -1, axis=0)
    present = jnp.arange(KEYFRAMES) < KEYFRAMES - 1

    def segment(operands):
        q_rows, k_rows, v_rows, left_k, left_v, right_k, right_v, has_right = operands
        keys = jnp.concatenate([left_k, k_rows, right_k], axis=0)
        vals = jnp.concatenate([left_v, v_rows, right_v], axis=0)
        valid = jnp.concatenate([jnp.ones((seg_rows + PL,), bool), jnp.full((PL,), has_right)])
        qh = head_split(q_rows)
        kh = head_split(keys)
        vh = head_split(vals)
        scores = jnp.einsum("hqd,hkd->hqk", qh, kh, precision=lax.Precision.HIGHEST) * factor
        scores = jnp.where(valid[None, None, :], scores, -1e30)
        peak = jnp.max(scores, axis=2, keepdims=True)
        weights = jnp.where(valid[None, None, :], jnp.exp(scores - peak), 0.0)
        total = jnp.sum(weights, axis=2, keepdims=True)
        rounded = lax.optimization_barrier(weights.astype(jnp.bfloat16)).astype(jnp.float32)
        result = jnp.einsum("hqk,hkd->hqd", rounded, vh, precision=lax.Precision.HIGHEST) / total
        return jnp.transpose(result, (1, 0, 2)).reshape(seg_rows, HEADS * HD).astype(jnp.bfloat16)

    local_out = lax.map(segment, (q_seg, k_seg, v_seg, a_k, a_v, r_k, r_v, present))
    return global_out, local_out.reshape(LOCAL_ROWS, HEADS * HD)
```

```python
import math

import jax
import jax.numpy as jnp
from jax import lax
from jax.experimental import pallas as pl
from jax.experimental.pallas import tpu as pltpu
from jax.sharding import PartitionSpec as P

HD = 128
HEADS = 8
PG = 32
PL = 88
ROWS = 968
KEYS = 1152
FULL = 1024
CHUNKS = (240, 240, 240, 248)
FLAG = 16
BLOCK = PG * HEADS
MESH = pl.DeviceIdType.MESH
LOG2 = math.log2(math.e) / math.sqrt(HD)
LOW = -1e30
bf16, f32 = jnp.bfloat16, jnp.float32


def spread(parts):
    shape = (HD, HD)
    diagonal = lax.broadcasted_iota(jnp.int32, shape, 0) == lax.broadcasted_iota(jnp.int32, shape, 1)
    wide = [jnp.where(diagonal, jnp.broadcast_to(part, shape), 0.0).astype(bf16) for part in parts]
    ones = jnp.ones((len(parts) * HD, HD), bf16)
    return jnp.dot(jnp.concatenate(wide, axis=1), ones, preferred_element_type=f32)


def split_rows(wide):
    shape = (HD, HD)
    diagonal = lax.broadcasted_iota(jnp.int32, shape, 0) == lax.broadcasted_iota(jnp.int32, shape, 1)
    row = lax.broadcasted_iota(jnp.int32, (FLAG, HD), 0)
    tile = jnp.zeros((FLAG, HD), f32)
    blocks = wide.shape[0] // HD
    for block in range(blocks):
        rest = jnp.sum(jnp.where(diagonal, wide[block * HD : (block + 1) * HD], 0.0), axis=0, keepdims=True)
        for part in range(3):
            piece = rest.astype(bf16).astype(f32)
            tile = jnp.where(row == part * blocks + block, jnp.broadcast_to(piece, tile.shape), tile)
            rest = rest - piece
    return tile.astype(bf16)


def kernel(
    gq, gk, gv, mask, wo, lq, lk, lv, ak, av, gout, lout,
    gq_v, gk_v, gv_v, gsrc, grecv, qb, kvb, qcat, kcat, vcat, psend, precv, asend, arecv,
    wo_v, msend, mrecv, qv, kv, vv, akv, avv, nkv, nvv, ov, kf, va,
    in_sem, head_sem, out_sem, a_send, a_recv, q_send, q_recv, k_send, k_recv, p_send, p_recv,
    o_send, o_recv, m_send, m_recv, n_send, n_recv,
):
    t, mp = lax.axis_index("tm"), lax.axis_index("mp")
    y, xl, za, zb, c = t // 32, (t // 16) % 2, (t // 4) % 4, (t // 2) % 2, t % 2
    g = xl * 4 + zb * 2 + c

    def place(y, xl, za, zb, c):
        return y * 32 + xl * 16 + za * 4 + zb * 2 + c

    members = []
    for rel in range(1, 8):
        x2, z2, c2 = (xl + rel // 4) % 2, (zb + rel // 2 % 2) % 2, (c + rel % 2) % 2
        members.append((rel, x2 * 4 + z2 * 2 + c2, place(y, x2, za, z2, c2)))
    along_z = [(d, place(y, xl, (za + d) % 4, zb, c)) for d in (1, 2, 3)]
    along_y = [(d, place((y + d) % 4, xl, za, zb, c)) for d in (1, 2, 3)]
    before = (t + 127) % 128
    other = (t + 127 + 2 * c) % 128

    barrier = pltpu.get_barrier_semaphore()
    partners = [m[2] for m in members] + [p for _, p in along_z] + [p for _, p in along_y] + [other]
    for partner in partners:
        pl.semaphore_signal(barrier, inc=1, device_id={"tm": partner, "mp": mp}, device_id_type=MESH)
    pl.semaphore_signal(barrier, inc=1, device_id={"tm": t, "mp": 1 - mp}, device_id_type=MESH)

    def remote(src, dst, send, recv, partner):
        return pltpu.make_async_remote_copy(
            src_ref=src, dst_ref=dst, send_sem=send, recv_sem=recv,
            device_id={"tm": partner, "mp": mp}, device_id_type=MESH,
        )

    def head_columns(h):
        return pl.ds(h * HD, HD)

    own = [pltpu.make_async_copy(src, dst, in_sem.at[i]) for i, (src, dst) in enumerate(((gq, gq_v), (gk, gk_v), (gv, gv_v)))]
    wo_copy = pltpu.make_async_copy(wo, wo_v, in_sem.at[3])

    def head_copies(h):
        pairs = ((lq, qv), (lk, kv), (lv, vv), (ak, akv), (av, avv))
        return [
            pltpu.make_async_copy(src.at[:, head_columns(h)], dst.at[h], head_sem.at[i, h])
            for i, (src, dst) in enumerate(pairs)
        ]

    def out_copy(h):
        return pltpu.make_async_copy(ov.at[h], lout.at[:, head_columns(h)], out_sem.at[h])

    def anchor_copies(h):
        return [
            remote(src.at[:, head_columns(h)], dst.at[h], n_send.at[i, h], n_recv.at[i, h], before)
            for i, (src, dst) in enumerate(((ak, nkv), (av, nvv)))
        ]

    def member_copies():
        return [remote(gsrc.at[m], grecv.at[g], a_send.at[rel], a_recv.at[rel], p) for rel, m, p in members]

    def spread_copies():
        return [remote(qb.at[za], qb.at[za], q_send.at[d], q_recv.at[d], p) for d, p in along_z] + [
            remote(kvb.at[y], kvb.at[y], k_send.at[d], k_recv.at[d], p) for d, p in along_y
        ]

    def partial_copy(d, p):
        return remote(psend.at[d], precv.at[za], p_send.at[d], p_recv.at[d], p)

    def attended_copies():
        return [remote(asend.at[m], arecv.at[g], o_send.at[rel], o_recv.at[rel], p) for rel, m, p in members]

    for copy in own:
        copy.start()
    for copy in head_copies(0):
        copy.start()

    def start_head(h, unused):
        for copy in head_copies(h):
            copy.start()
        return unused

    lax.fori_loop(1, HEADS, start_head, 0)
    wo_copy.start()

    given = jnp.full((FLAG, 3 * HD), mask[0].astype(f32), f32).astype(bf16)
    for copy in own:
        copy.wait()
    for h in range(HEADS):
        columns = slice(h * HD, (h + 1) * HD)
        gsrc[h, :PG, :HD] = gq_v[:, columns]
        gsrc[h, :PG, HD : 2 * HD] = gk_v[:, columns]
        gsrc[h, :PG, 2 * HD :] = gv_v[:, columns]
        gsrc[h, PG:, :] = given
    grecv[g] = gsrc[g]
    va[:, HD:] = jnp.ones((KEYS, HD), bf16)
    vcat[:, HD:] = jnp.ones((4 * BLOCK, HD), bf16)

    pl.semaphore_wait(barrier, len(partners) + 1)
    for copy in member_copies():
        copy.start()

    def start_anchor(h, unused):
        for copy in anchor_copies(h):
            copy.start()
        return unused

    lax.fori_loop(0, HEADS, start_anchor, 0)

    def gather_blocks():
        for copy in member_copies():
            copy.wait_recv()
        row = lax.broadcasted_iota(jnp.int32, (FLAG, HD), 0)
        flags = jnp.zeros((FLAG, HD), f32)
        for m in range(HEADS):
            qb[za, m * PG : (m + 1) * PG, :] = grecv[m, :PG, :HD]
            kvb[y, m * PG : (m + 1) * PG, :] = grecv[m, :PG, HD:]
            flags = jnp.where(row == m, grecv[m, PG:, :HD].astype(f32), flags)
        flags = flags.astype(bf16)
        qb[za, BLOCK:, :] = flags
        kvb[y, BLOCK:, :HD] = flags
        kvb[y, BLOCK:, HD:] = flags
        for copy in spread_copies():
            copy.start()

    def keyframe_attention():
        for copy in spread_copies():
            copy.wait_recv()
        first = lax.broadcasted_iota(jnp.int32, (PG, HD), 1) == 0
        for s in range(4):
            rows = slice(s * BLOCK, (s + 1) * BLOCK)
            qcat[rows, :HD] = qb[s, :BLOCK, :]
            kcat[rows, :HD] = kvb[s, :BLOCK, :HD]
            vcat[rows, :HD] = kvb[s, :BLOCK, HD:]
            q_flags = qb[s, BLOCK:, :].astype(f32)
            k_flags = kvb[s, BLOCK:, :HD].astype(f32)
            for m in range(HEADS):
                part = slice(s * BLOCK + m * PG, s * BLOCK + (m + 1) * PG)
                q_flag = jnp.broadcast_to(q_flags[m : m + 1, :], (PG, HD))
                k_flag = jnp.broadcast_to(k_flags[m : m + 1, :], (PG, HD))
                qcat[part, HD:] = jnp.where(first, q_flag, 0.0).astype(bf16)
                kcat[part, HD:] = jnp.where(first, (k_flag - 1.0) * -LOW, 0.0).astype(bf16)
        for d in (2, 1, 3, 0):
            rows = pl.ds(pl.multiple_of((za + d) % 4 * BLOCK, BLOCK), BLOCK)
            scores = lax.dot_general(
                qcat[rows, :], kcat[...], (((1,), (1,)), ((), ())), preferred_element_type=f32
            )
            peak = jnp.max(scores, axis=1, keepdims=True)
            weights = jnp.exp2((scores - peak) * LOG2).astype(bf16)
            summed = jnp.dot(weights, vcat[...], preferred_element_type=f32)
            total = summed[:, HD:]
            mean = (summed[:, :HD] / total).astype(bf16)
            tile = split_rows(peak * LOG2 + jnp.log2(total))
            if d == 0:
                precv[za, :BLOCK, :] = mean
                precv[za, BLOCK:, :] = tile
            else:
                psend[d, :BLOCK, :] = mean
                psend[d, BLOCK:, :] = tile
                partial_copy(d, along_z[d - 1][1]).start()

    def combine_partials():
        for d, p in along_z:
            partial_copy(d, p).wait_recv()
        for block in range(BLOCK // HD):
            rows = slice(block * HD, (block + 1) * HD)
            logs = []
            for s in range(4):
                tile = precv[s, BLOCK:, :].astype(f32)
                logs.append(spread([tile[2 * part + block : 2 * part + block + 1, :] for part in range(3)]))
            peak = jnp.maximum(jnp.maximum(logs[0], logs[1]), jnp.maximum(logs[2], logs[3]))
            total = jnp.zeros((HD, HD), f32)
            summed = jnp.zeros((HD, HD), f32)
            for s in range(4):
                share = jnp.exp2(logs[s] - peak)
                total = total + share
                summed = summed + share * precv[s, rows, :].astype(f32)
            attended = (summed / total).astype(bf16)
            for m in range(HD // PG):
                asend[block * (HD // PG) + m] = attended[m * PG : (m + 1) * PG, :]
        arecv[g] = asend[g]
        for copy in attended_copies():
            copy.start()

    def project():
        for copy in attended_copies():
            copy.wait_recv()
        wo_copy.wait()
        attended = jnp.concatenate([arecv[h] for h in range(HEADS)], axis=1)
        half = HEADS * HD
        theirs = pl.ds(pl.multiple_of((1 - mp) * half, half), half)
        mine = pl.ds(pl.multiple_of(mp * half, half), half)
        msend[...] = jnp.dot(attended, wo_v[:, theirs], preferred_element_type=f32).astype(bf16)
        swap = pltpu.make_async_remote_copy(
            src_ref=msend, dst_ref=mrecv, send_sem=m_send, recv_sem=m_recv,
            device_id={"tm": t, "mp": 1 - mp}, device_id_type=MESH,
        )
        swap.start()
        kept = jnp.dot(attended, wo_v[:, mine], preferred_element_type=f32)
        swap.wait()
        gout[...] = (kept + mrecv[...].astype(f32)).astype(bf16)

    valid = jnp.where(t == 127, ROWS + PL, ROWS + 2 * PL) - FULL

    def local_scores(h, start, rows):
        q = (qv[h, start : start + rows, :].astype(f32) * LOG2).astype(bf16)
        scores = lax.dot_general(q, kf[...], (((1,), (1,)), ((), ())), preferred_element_type=f32)
        last = scores[:, FULL:]
        lane = lax.broadcasted_iota(jnp.int32, last.shape, 1)
        return jnp.concatenate([scores[:, :FULL], jnp.where(lane < valid, last, LOW)], axis=1)

    def local_head(h, unused):
        pl.when(h == 1)(gather_blocks)
        pl.when(h == 6)(keyframe_attention)
        for copy in head_copies(h):
            copy.wait()
        for copy in anchor_copies(h):
            copy.wait_recv()
        pad = jnp.zeros((KEYS - ROWS - 2 * PL, HD), f32)
        kf[...] = jnp.concatenate([x[h].astype(f32) for x in (kv, akv, nkv)] + [pad], axis=0).astype(bf16)
        va[:, :HD] = jnp.concatenate([x[h].astype(f32) for x in (vv, avv, nvv)] + [pad], axis=0).astype(bf16)
        starts = [sum(CHUNKS[:i]) for i in range(len(CHUNKS))]
        scores = local_scores(h, starts[0], CHUNKS[0])
        for i, (start, rows) in enumerate(zip(starts, CHUNKS)):
            now = scores
            if i + 1 < len(CHUNKS):
                scores = local_scores(h, starts[i + 1], CHUNKS[i + 1])
            peak = jnp.max(now, axis=1, keepdims=True)
            weights = jnp.exp2((now - peak).astype(bf16))
            summed = jnp.dot(weights, va[...], preferred_element_type=f32)
            ov[h, start : start + rows, :] = (summed[:, :HD] / summed[:, HD:]).astype(bf16)
        out_copy(h).start()
        return unused

    lax.fori_loop(0, HEADS, local_head, 0)
    combine_partials()
    project()

    def finish(h, unused):
        out_copy(h).wait()
        for copy in anchor_copies(h):
            copy.wait_send()
        return unused

    lax.fori_loop(0, HEADS, finish, 0)
    for copy in member_copies() + spread_copies() + [partial_copy(d, p) for d, p in along_z] + attended_copies():
        copy.wait_send()


def body(*args):
    dma = pltpu.SemaphoreType.DMA
    vmem = lambda *shape: pltpu.VMEM(shape, bf16)
    anywhere = pl.BlockSpec(memory_space=pl.ANY)
    width = HEADS * HD
    return pl.pallas_call(
        kernel,
        name="keyframe_and_infill",
        out_shape=(
            jax.ShapeDtypeStruct((PG, width), bf16),
            jax.ShapeDtypeStruct((ROWS, width), bf16),
        ),
        in_specs=[anywhere] * 3 + [pl.BlockSpec(memory_space=pltpu.SMEM)] + [anywhere] * 6,
        out_specs=(pl.BlockSpec(memory_space=pltpu.VMEM), anywhere),
        scratch_shapes=[
            vmem(PG, width), vmem(PG, width), vmem(PG, width),
            vmem(HEADS, PG + FLAG, 3 * HD), vmem(HEADS, PG + FLAG, 3 * HD),
            vmem(4, BLOCK + FLAG, HD), vmem(4, BLOCK + FLAG, 2 * HD),
            vmem(4 * BLOCK, 2 * HD), vmem(4 * BLOCK, 2 * HD), vmem(4 * BLOCK, 2 * HD),
            vmem(4, BLOCK + FLAG, HD), vmem(4, BLOCK + FLAG, HD),
            vmem(HEADS, PG, HD), vmem(HEADS, PG, HD),
            vmem(width, 2 * width), vmem(PG, width), vmem(PG, width),
            vmem(HEADS, ROWS, HD), vmem(HEADS, ROWS, HD), vmem(HEADS, ROWS, HD),
            vmem(HEADS, PL, HD), vmem(HEADS, PL, HD), vmem(HEADS, PL, HD), vmem(HEADS, PL, HD),
            vmem(HEADS, ROWS, HD), vmem(KEYS, HD), vmem(KEYS, 2 * HD),
            dma((4,)), dma((5, HEADS)), dma((HEADS,)),
            dma((8,)), dma((8,)), dma((4,)), dma((4,)), dma((4,)), dma((4,)), dma((4,)), dma((4,)),
            dma((8,)), dma((8,)), dma, dma, dma((2, HEADS)), dma((2, HEADS)),
        ],
        compiler_params=pltpu.CompilerParams(
            collective_id=1, has_side_effects=True, vmem_limit_bytes=60 * 2**20
        ),
    )(*args)


def solution(mesh):
    whole, rows = P("tm", "mp"), P("mp", None)
    return jax.shard_map(
        body,
        mesh=mesh,
        in_specs=(whole, whole, whole, P("tm"), rows) + (whole,) * 5,
        out_specs=(whole, whole),
        check_vma=False,
    )
```

```python
import math

import jax
import jax.numpy as jnp
from jax import lax
from jax.experimental import pallas as pl
from jax.experimental.pallas import tpu as pltpu
from jax.sharding import PartitionSpec as P

HD = 128
HEADS = 8
PG = 32
PL = 88
ROWS = 968
KEYS = 1152
FULL = 1024
CHUNKS = (240, 240, 240, 248)
FLAG = 16
BLOCK = PG * HEADS
MESH = pl.DeviceIdType.MESH
LOG2 = math.log2(math.e) / math.sqrt(HD)
LOW = -1e30
bf16, f32 = jnp.bfloat16, jnp.float32


def spread(parts):
    shape = (HD, HD)
    diagonal = lax.broadcasted_iota(jnp.int32, shape, 0) == lax.broadcasted_iota(jnp.int32, shape, 1)
    wide = [jnp.where(diagonal, jnp.broadcast_to(part, shape), 0.0).astype(bf16) for part in parts]
    ones = jnp.ones((len(parts) * HD, HD), bf16)
    return jnp.dot(jnp.concatenate(wide, axis=1), ones, preferred_element_type=f32)


def split_rows(wide):
    shape = (HD, HD)
    diagonal = lax.broadcasted_iota(jnp.int32, shape, 0) == lax.broadcasted_iota(jnp.int32, shape, 1)
    row = lax.broadcasted_iota(jnp.int32, (FLAG, HD), 0)
    tile = jnp.zeros((FLAG, HD), f32)
    blocks = wide.shape[0] // HD
    for block in range(blocks):
        rest = jnp.sum(jnp.where(diagonal, wide[block * HD : (block + 1) * HD], 0.0), axis=0, keepdims=True)
        for part in range(3):
            piece = rest.astype(bf16).astype(f32)
            tile = jnp.where(row == part * blocks + block, jnp.broadcast_to(piece, tile.shape), tile)
            rest = rest - piece
    return tile.astype(bf16)


def kernel(
    gq, gk, gv, mask, wo, lq, lk, lv, ak, av, att, wo_other, wo_mine, lout,
    gq_v, gk_v, gv_v, gsrc, grecv, qb, kvb, qcat, kcat, vcat, psend, precv, asend, qv, kv, vv, akv, avv, nkv, nvv, ov, kf, va,
    in_sem, head_sem, out_sem, a_send, a_recv, q_send, q_recv, k_send, k_recv, p_send, p_recv,
    o_send, o_recv, w_send, w_recv, n_send, n_recv,
):
    t, mp = lax.axis_index("tm"), lax.axis_index("mp")
    y, xl, za, zb, c = t // 32, (t // 16) % 2, (t // 4) % 4, (t // 2) % 2, t % 2
    g = xl * 4 + zb * 2 + c

    def place(y, xl, za, zb, c):
        return y * 32 + xl * 16 + za * 4 + zb * 2 + c

    group = []
    for rel in range(8):
        x2, z2, c2 = (xl + rel // 4) % 2, (zb + rel // 2 % 2) % 2, (c + rel % 2) % 2
        group.append((rel, x2 * 4 + z2 * 2 + c2, place(y, x2, za, z2, c2)))
    members = group[1:]
    across = place(y, 1 - xl, za, zb, c)
    sibling = place(y, xl, za, zb, 1 - c)
    along_z = [(d, place(y, xl, (za + d) % 4, zb, c)) for d in (1, 2, 3)]
    along_y = [(d, place((y + d) % 4, xl, za, zb, c)) for d in (1, 2, 3)]
    before = (t + 127) % 128
    other = (t + 127 + 2 * c) % 128

    barrier = pltpu.get_barrier_semaphore()
    partners = [m[2] for m in members] + [p for _, p in along_z] + [p for _, p in along_y] + [other]
    partners = [(p, mp) for p in partners] + [(m[2], 1 - mp) for m in group]
    for partner, side in partners:
        pl.semaphore_signal(barrier, inc=1, device_id={"tm": partner, "mp": side}, device_id_type=MESH)

    def remote(src, dst, send, recv, partner, side=mp):
        return pltpu.make_async_remote_copy(
            src_ref=src, dst_ref=dst, send_sem=send, recv_sem=recv,
            device_id={"tm": partner, "mp": side}, device_id_type=MESH,
        )

    def head_columns(h):
        return pl.ds(h * HD, HD)

    own = [pltpu.make_async_copy(src, dst, in_sem.at[i]) for i, (src, dst) in enumerate(((gq, gq_v), (gk, gk_v), (gv, gv_v)))]

    def head_copies(h):
        pairs = ((lq, qv), (lk, kv), (lv, vv), (ak, akv), (av, avv))
        return [
            pltpu.make_async_copy(src.at[:, head_columns(h)], dst.at[h], head_sem.at[i, h])
            for i, (src, dst) in enumerate(pairs)
        ]

    def out_copy(h):
        return pltpu.make_async_copy(ov.at[h], lout.at[h], out_sem.at[h])

    def anchor_copies(h):
        return [
            remote(src.at[:, head_columns(h)], dst.at[h], n_send.at[i, h], n_recv.at[i, h], before)
            for i, (src, dst) in enumerate(((ak, nkv), (av, nvv)))
        ]

    def member_copies():
        return [remote(gsrc.at[m], grecv.at[g], a_send.at[rel], a_recv.at[rel], p) for rel, m, p in members]

    def spread_copies():
        return [remote(qb.at[za], qb.at[za], q_send.at[d], q_recv.at[d], p) for d, p in along_z] + [
            remote(kvb.at[y], kvb.at[y], k_send.at[d], k_recv.at[d], p) for d, p in along_y
        ]

    def partial_copy(d, p):
        return remote(psend.at[d], precv.at[za], p_send.at[d], p_recv.at[d], p)

    def attended_copies():
        slot = att.at[mp * HEADS + g]
        return [
            remote(asend.at[m], slot, o_send.at[rel + 8 * i], o_recv.at[rel + 8 * i], p, side)
            for i, side in enumerate((mp, 1 - mp))
            for rel, m, p in group[1 - i :]
        ]

    half = HEADS * HD
    own_half = pl.ds(pl.multiple_of(c * (half // 2), half // 2), half // 2)

    def wo_across():
        src = wo.at[own_half, pl.ds(pl.multiple_of((1 - mp) * half, half), half)]
        return remote(src, wo_other.at[own_half, :], w_send.at[0], w_recv.at[0], across, 1 - mp)

    def wo_beside():
        rows = wo_other.at[own_half, :]
        return remote(rows, rows, w_send.at[1], w_recv.at[1], sibling)

    mine = pl.ds(pl.multiple_of(mp * half, half), half)
    wo_copy = pltpu.make_async_copy(wo.at[:, mine], wo_mine, in_sem.at[4])
    own_slot = pltpu.make_async_copy(asend.at[g], att.at[mp * HEADS + g], in_sem.at[3])

    for copy in own:
        copy.start()
    for copy in head_copies(0):
        copy.start()

    def start_head(h, unused):
        for copy in head_copies(h):
            copy.start()
        return unused

    lax.fori_loop(1, HEADS, start_head, 0)
    wo_copy.start()

    given = jnp.full((FLAG, 3 * HD), mask[0].astype(f32), f32).astype(bf16)
    for copy in own:
        copy.wait()
    for h in range(HEADS):
        columns = slice(h * HD, (h + 1) * HD)
        gsrc[h, :PG, :HD] = gq_v[:, columns]
        gsrc[h, :PG, HD : 2 * HD] = gk_v[:, columns]
        gsrc[h, :PG, 2 * HD :] = gv_v[:, columns]
        gsrc[h, PG:, :] = given
    grecv[g] = gsrc[g]
    va[:, HD:] = jnp.ones((KEYS, HD), bf16)
    vcat[:, HD:] = jnp.ones((4 * BLOCK, HD), bf16)

    pl.semaphore_wait(barrier, len(partners))
    for copy in member_copies():
        copy.start()

    def start_anchor(h, unused):
        for copy in anchor_copies(h):
            copy.start()
        return unused

    lax.fori_loop(0, HEADS, start_anchor, 0)
    wo_across().start()

    def gather_blocks():
        for copy in member_copies():
            copy.wait_recv()
        row = lax.broadcasted_iota(jnp.int32, (FLAG, HD), 0)
        flags = jnp.zeros((FLAG, HD), f32)
        for m in range(HEADS):
            qb[za, m * PG : (m + 1) * PG, :] = grecv[m, :PG, :HD]
            kvb[y, m * PG : (m + 1) * PG, :] = grecv[m, :PG, HD:]
            flags = jnp.where(row == m, grecv[m, PG:, :HD].astype(f32), flags)
        flags = flags.astype(bf16)
        qb[za, BLOCK:, :] = flags
        kvb[y, BLOCK:, :HD] = flags
        kvb[y, BLOCK:, HD:] = flags
        for copy in spread_copies():
            copy.start()

    def keyframe_attention():
        for copy in spread_copies():
            copy.wait_recv()
        first = lax.broadcasted_iota(jnp.int32, (PG, HD), 1) == 0
        for s in range(4):
            rows = slice(s * BLOCK, (s + 1) * BLOCK)
            qcat[rows, :HD] = qb[s, :BLOCK, :]
            kcat[rows, :HD] = kvb[s, :BLOCK, :HD]
            vcat[rows, :HD] = kvb[s, :BLOCK, HD:]
            q_flags = qb[s, BLOCK:, :].astype(f32)
            k_flags = kvb[s, BLOCK:, :HD].astype(f32)
            for m in range(HEADS):
                part = slice(s * BLOCK + m * PG, s * BLOCK + (m + 1) * PG)
                q_flag = jnp.broadcast_to(q_flags[m : m + 1, :], (PG, HD))
                k_flag = jnp.broadcast_to(k_flags[m : m + 1, :], (PG, HD))
                qcat[part, HD:] = jnp.where(first, q_flag, 0.0).astype(bf16)
                kcat[part, HD:] = jnp.where(first, (k_flag - 1.0) * -LOW, 0.0).astype(bf16)
        for d in (2, 1, 3, 0):
            rows = pl.ds(pl.multiple_of((za + d) % 4 * BLOCK, BLOCK), BLOCK)
            scores = lax.dot_general(
                qcat[rows, :], kcat[...], (((1,), (1,)), ((), ())), preferred_element_type=f32
            )
            peak = jnp.max(scores, axis=1, keepdims=True)
            weights = jnp.exp2((scores - peak) * LOG2).astype(bf16)
            summed = jnp.dot(weights, vcat[...], preferred_element_type=f32)
            total = summed[:, HD:]
            mean = (summed[:, :HD] / total).astype(bf16)
            tile = split_rows(peak * LOG2 + jnp.log2(total))
            if d == 0:
                precv[za, :BLOCK, :] = mean
                precv[za, BLOCK:, :] = tile
            else:
                psend[d, :BLOCK, :] = mean
                psend[d, BLOCK:, :] = tile
                partial_copy(d, along_z[d - 1][1]).start()

    def combine_partials():
        for d, p in along_z:
            partial_copy(d, p).wait_recv()
        for block in range(BLOCK // HD):
            rows = slice(block * HD, (block + 1) * HD)
            logs = []
            for s in range(4):
                tile = precv[s, BLOCK:, :].astype(f32)
                logs.append(spread([tile[2 * part + block : 2 * part + block + 1, :] for part in range(3)]))
            peak = jnp.maximum(jnp.maximum(logs[0], logs[1]), jnp.maximum(logs[2], logs[3]))
            total = jnp.zeros((HD, HD), f32)
            summed = jnp.zeros((HD, HD), f32)
            for s in range(4):
                share = jnp.exp2(logs[s] - peak)
                total = total + share
                summed = summed + share * precv[s, rows, :].astype(f32)
            attended = (summed / total).astype(bf16)
            for m in range(HD // PG):
                asend[block * (HD // PG) + m] = attended[m * PG : (m + 1) * PG, :]
        for copy in attended_copies():
            copy.start()
        own_slot.start()
        wo_across().wait_recv()
        wo_beside().start()

    valid = jnp.where(t == 127, ROWS + PL, ROWS + 2 * PL) - FULL

    def local_scores(h, start, rows):
        q = (qv[h, start : start + rows, :].astype(f32) * LOG2).astype(bf16)
        scores = lax.dot_general(q, kf[...], (((1,), (1,)), ((), ())), preferred_element_type=f32)
        last = scores[:, FULL:]
        lane = lax.broadcasted_iota(jnp.int32, last.shape, 1)
        return jnp.concatenate([scores[:, :FULL], jnp.where(lane < valid, last, LOW)], axis=1)

    def local_head(h, unused):
        pl.when(h == 4)(keyframe_attention)
        pl.when(h == 7)(combine_partials)
        for copy in head_copies(h):
            copy.wait()
        for copy in anchor_copies(h):
            copy.wait_recv()
        pad = jnp.zeros((KEYS - ROWS - 2 * PL, HD), f32)
        kf[...] = jnp.concatenate([x[h].astype(f32) for x in (kv, akv, nkv)] + [pad], axis=0).astype(bf16)
        va[:, :HD] = jnp.concatenate([x[h].astype(f32) for x in (vv, avv, nvv)] + [pad], axis=0).astype(bf16)
        starts = [sum(CHUNKS[:i]) for i in range(len(CHUNKS))]
        scores = local_scores(h, starts[0], CHUNKS[0])
        for i, (start, rows) in enumerate(zip(starts, CHUNKS)):
            now = scores
            if i + 1 < len(CHUNKS):
                scores = local_scores(h, starts[i + 1], CHUNKS[i + 1])
            peak = jnp.max(now, axis=1, keepdims=True)
            weights = jnp.exp2((now - peak).astype(bf16))
            summed = jnp.dot(weights, va[...], preferred_element_type=f32)
            ov[h, start : start + rows, :] = (summed[:, :HD] / summed[:, HD:]).astype(bf16)
        out_copy(h).start()
        return unused

    gather_blocks()
    lax.fori_loop(0, HEADS, local_head, 0)

    def finish(h, unused):
        out_copy(h).wait()
        for copy in anchor_copies(h):
            copy.wait_send()
        return unused

    lax.fori_loop(0, HEADS, finish, 0)
    for copy in member_copies() + spread_copies() + [partial_copy(d, p) for d, p in along_z]:
        copy.wait_send()
    for copy in attended_copies() + [wo_beside()]:
        copy.wait()
    wo_across().wait_send()
    own_slot.wait()
    wo_copy.wait()


def project_kernel(att, wo_mine, wo_other, heads, gout, lout, out_sem):
    mp = lax.axis_index("mp")
    moves = [
        pltpu.make_async_copy(heads.at[h], lout.at[:, pl.ds(h * HD, HD)], out_sem.at[h]) for h in range(HEADS)
    ]
    for move in moves:
        move.start()
    total = jnp.zeros(gout.shape, f32)
    for side, wo in ((mp, wo_mine), (1 - mp, wo_other)):
        attended = jnp.concatenate([att[side * HEADS + h] for h in range(HEADS)], axis=1)
        total = total + jnp.dot(attended, wo[...], preferred_element_type=f32)
    gout[...] = total.astype(bf16)
    for move in moves:
        move.wait()


def body(*args):
    dma = pltpu.SemaphoreType.DMA
    vmem = lambda *shape: pltpu.VMEM(shape, bf16)
    anywhere = pl.BlockSpec(memory_space=pl.ANY)
    in_vmem = pl.BlockSpec(memory_space=pltpu.VMEM)
    width = HEADS * HD
    att, wo_other, wo_mine, heads = pl.pallas_call(
        kernel,
        name="keyframe_and_infill",
        out_shape=(vmem(2 * HEADS, PG, HD), vmem(width, width), vmem(width, width), vmem(HEADS, ROWS, HD)),
        in_specs=[anywhere] * 3 + [pl.BlockSpec(memory_space=pltpu.SMEM)] + [anywhere] * 6,
        out_specs=(anywhere,) * 4,
        scratch_shapes=[
            vmem(PG, width), vmem(PG, width), vmem(PG, width),
            vmem(HEADS, PG + FLAG, 3 * HD), vmem(HEADS, PG + FLAG, 3 * HD),
            vmem(4, BLOCK + FLAG, HD), vmem(4, BLOCK + FLAG, 2 * HD),
            vmem(4 * BLOCK, 2 * HD), vmem(4 * BLOCK, 2 * HD), vmem(4 * BLOCK, 2 * HD),
            vmem(4, BLOCK + FLAG, HD), vmem(4, BLOCK + FLAG, HD), vmem(HEADS, PG, HD),
            vmem(HEADS, ROWS, HD), vmem(HEADS, ROWS, HD), vmem(HEADS, ROWS, HD),
            vmem(HEADS, PL, HD), vmem(HEADS, PL, HD), vmem(HEADS, PL, HD), vmem(HEADS, PL, HD),
            vmem(HEADS, ROWS, HD), vmem(KEYS, HD), vmem(KEYS, 2 * HD),
            dma((5,)), dma((5, HEADS)), dma((HEADS,)),
            dma((8,)), dma((8,)), dma((4,)), dma((4,)), dma((4,)), dma((4,)), dma((4,)), dma((4,)),
            dma((16,)), dma((16,)), dma((2,)), dma((2,)), dma((2, HEADS)), dma((2, HEADS)),
        ],
        compiler_params=pltpu.CompilerParams(
            collective_id=1, has_side_effects=True, vmem_limit_bytes=44 * 2**20
        ),
    )(*[arg if arg.ndim == 1 else pltpu.with_memory_space_constraint(arg, pltpu.HBM) for arg in args])
    return pl.pallas_call(
        project_kernel,
        name="projection",
        out_shape=(
            jax.ShapeDtypeStruct((PG, width), bf16),
            jax.ShapeDtypeStruct((ROWS, width), bf16),
        ),
        in_specs=[in_vmem] * 3 + [anywhere],
        out_specs=(in_vmem, anywhere),
        scratch_shapes=[dma((HEADS,))],
        compiler_params=pltpu.CompilerParams(vmem_limit_bytes=8 * 2**20),
    )(att, wo_mine, wo_other, heads)


def solution(mesh):
    whole, rows = P("tm", "mp"), P("mp", None)
    return jax.shard_map(
        body,
        mesh=mesh,
        in_specs=(whole, whole, whole, P("tm"), rows) + (whole,) * 5,
        out_specs=(whole, whole),
        check_vma=False,
    )
```

```python
import math

import jax
import jax.numpy as jnp
from jax import lax
from jax.experimental import pallas as pl
from jax.experimental.pallas import tpu as pltpu
from jax.sharding import PartitionSpec as P

HD = 128
HEADS = 8
PG = 32
PL = 88
ROWS = 968
KEYS = 1152
FULL = 1024
CHUNKS = (240, 240, 240, 248)
FLAG = 16
BLOCK = PG * HEADS
MESH = pl.DeviceIdType.MESH
LOG2 = math.log2(math.e) / math.sqrt(HD)
LOW = -1e30
bf16, f32 = jnp.bfloat16, jnp.float32


def spread(parts):
    shape = (HD, HD)
    diagonal = lax.broadcasted_iota(jnp.int32, shape, 0) == lax.broadcasted_iota(jnp.int32, shape, 1)
    wide = [jnp.where(diagonal, jnp.broadcast_to(part, shape), 0.0).astype(bf16) for part in parts]
    ones = jnp.ones((len(parts) * HD, HD), bf16)
    return jnp.dot(jnp.concatenate(wide, axis=1), ones, preferred_element_type=f32)


def split_rows(wide):
    shape = (HD, HD)
    diagonal = lax.broadcasted_iota(jnp.int32, shape, 0) == lax.broadcasted_iota(jnp.int32, shape, 1)
    row = lax.broadcasted_iota(jnp.int32, (FLAG, HD), 0)
    tile = jnp.zeros((FLAG, HD), f32)
    blocks = wide.shape[0] // HD
    for block in range(blocks):
        rest = jnp.sum(jnp.where(diagonal, wide[block * HD : (block + 1) * HD], 0.0), axis=0, keepdims=True)
        for part in range(3):
            piece = rest.astype(bf16).astype(f32)
            tile = jnp.where(row == part * blocks + block, jnp.broadcast_to(piece, tile.shape), tile)
            rest = rest - piece
    return tile.astype(bf16)


def kernel(
    gq, gk, gv, mask, wo, lq, lk, lv, ak, av, att, wo_other, wo_mine, lout,
    gq_v, gk_v, gv_v, gsrc, grecv, qb, kb, qcat, kcat, vcat, wcat, psend, precv, asend, qv, kv, vv, akv, avv, nkv, nvv, ov, kf, va,
    in_sem, head_sem, out_sem, a_send, a_recv, q_send, q_recv, k_send, k_recv, v_send, v_recv, p_send, p_recv,
    o_send, o_recv, w_send, w_recv, n_send, n_recv,
):
    t, mp = lax.axis_index("tm"), lax.axis_index("mp")
    y, xl, za, zb, c = t // 32, (t // 16) % 2, (t // 4) % 4, (t // 2) % 2, t % 2
    g = xl * 4 + zb * 2 + c

    def place(y, xl, za, zb, c):
        return y * 32 + xl * 16 + za * 4 + zb * 2 + c

    group = []
    for rel in range(8):
        x2, z2, c2 = (xl + rel // 4) % 2, (zb + rel // 2 % 2) % 2, (c + rel % 2) % 2
        group.append((rel, x2 * 4 + z2 * 2 + c2, place(y, x2, za, z2, c2)))
    members = group[1:]
    across = place(y, 1 - xl, za, zb, c)
    sibling = place(y, xl, za, zb, 1 - c)
    along_z = [(d, place(y, xl, (za + d) % 4, zb, c)) for d in (1, 2, 3)]
    along_y = [(d, place((y + d) % 4, xl, za, zb, c)) for d in (1, 2, 3)]
    before = (t + 127) % 128
    other = (t + 127 + 2 * c) % 128

    own = [
        pltpu.make_async_copy(src, dst, in_sem.at[i])
        for i, (src, dst) in enumerate(((gq, gq_v), (gk, gk_v), (gv, gv_v)))
    ]
    for copy in own:
        copy.start()

    barrier = pltpu.get_barrier_semaphore()
    partners = [(along_z[d][1], mp) for d in (1, 0, 2)] + [(along_y[d][1], mp) for d in (1, 0, 2)]
    partners += [(m[2], mp) for m in members[::-1]] + [(other, mp)] + [(m[2], 1 - mp) for m in group]
    for partner, side in partners:
        pl.semaphore_signal(barrier, inc=1, device_id={"tm": partner, "mp": side}, device_id_type=MESH)

    def remote(src, dst, send, recv, partner, side=mp):
        return pltpu.make_async_remote_copy(
            src_ref=src, dst_ref=dst, send_sem=send, recv_sem=recv,
            device_id={"tm": partner, "mp": side}, device_id_type=MESH,
        )

    def head_columns(h):
        return pl.ds(h * HD, HD)

    def head_copies(h):
        pairs = ((lq, qv), (lk, kv), (lv, vv), (ak, akv), (av, avv))
        return [
            pltpu.make_async_copy(src.at[:, head_columns(h)], dst.at[h], head_sem.at[i, h])
            for i, (src, dst) in enumerate(pairs)
        ]

    def out_copy(h):
        return pltpu.make_async_copy(ov.at[h], lout.at[:, head_columns(h)], out_sem.at[h])

    def anchor_copies(h):
        return [
            remote(src.at[:, head_columns(h)], dst.at[h], n_send.at[i, h], n_recv.at[i, h], before)
            for i, (src, dst) in enumerate(((ak, nkv), (av, nvv)))
        ]

    def member_copies():
        return [remote(gsrc.at[m], grecv.at[g], a_send.at[rel], a_recv.at[rel], p) for rel, m, p in members]

    def scores_copies():
        return [remote(qb.at[za], qb.at[za], q_send.at[d], q_recv.at[d], along_z[d - 1][1]) for d in (2, 1, 3)] + [
            remote(kb.at[y], kb.at[y], k_send.at[d], k_recv.at[d], along_y[d - 1][1]) for d in (2, 1, 3)
        ]

    def values_copies():
        rows = vcat.at[pl.ds(pl.multiple_of(y * BLOCK, BLOCK), BLOCK), :HD]
        return [remote(rows, rows, v_send.at[d], v_recv.at[d], along_y[d - 1][1]) for d in (2, 1, 3)]

    def partial_copy(d, p):
        return remote(psend.at[d], precv.at[za], p_send.at[d], p_recv.at[d], p)

    def attended_copies():
        slot = att.at[mp * HEADS + g]
        return [
            remote(asend.at[m], slot, o_send.at[rel + 8 * i], o_recv.at[rel + 8 * i], p, side)
            for i, side in ((1, 1 - mp), (0, mp))
            for rel, m, p in members[::-1] + group[:i]
        ]

    half = HEADS * HD
    own_half = pl.ds(pl.multiple_of(c * (half // 2), half // 2), half // 2)

    def wo_across():
        src = wo.at[own_half, pl.ds(pl.multiple_of((1 - mp) * half, half), half)]
        return remote(src, wo_other.at[own_half, :], w_send.at[0], w_recv.at[0], across, 1 - mp)

    def wo_beside():
        rows = wo_other.at[own_half, :]
        return remote(rows, rows, w_send.at[1], w_recv.at[1], sibling)

    mine = pl.ds(pl.multiple_of(mp * half, half), half)
    wo_copy = pltpu.make_async_copy(wo.at[:, mine], wo_mine, in_sem.at[5])
    own_slot = pltpu.make_async_copy(asend.at[g], att.at[mp * HEADS + g], in_sem.at[4])

    for copy in own:
        copy.wait()
    given = jnp.full((FLAG, HD), mask[0].astype(f32), f32).astype(bf16)
    for h in range(HEADS):
        columns = slice(h * HD, (h + 1) * HD)
        gsrc[h, :PG, :] = gq_v[:, columns]
        gsrc[h, PG : 2 * PG, :] = gk_v[:, columns]
        gsrc[h, 2 * PG : 3 * PG, :] = gv_v[:, columns]
        gsrc[h, 3 * PG :, :] = given
    pl.semaphore_wait(barrier, len(partners))
    for copy in member_copies()[::-1]:
        copy.start()

    def start_head(h, unused):
        for copy in anchor_copies(h) + head_copies(h):
            copy.start()
        return unused

    lax.fori_loop(0, HEADS, start_head, 0)
    wo_across().start()
    wo_copy.start()
    grecv[g] = gsrc[g]
    va[:, HD:] = jnp.ones((KEYS, HD), bf16)
    vcat[:, HD:] = jnp.ones((4 * BLOCK, HD), bf16)

    def gather_blocks():
        for copy in member_copies():
            copy.wait_recv()
        row = lax.broadcasted_iota(jnp.int32, (FLAG, HD), 0)
        flags = jnp.zeros((FLAG, HD), f32)
        for m in range(HEADS):
            rows = slice(m * PG, (m + 1) * PG)
            qb[za, rows, :] = grecv[m, :PG, :]
            kb[y, rows, :] = grecv[m, PG : 2 * PG, :]
            vcat[pl.ds(pl.multiple_of(y * BLOCK + m * PG, PG), PG), :HD] = grecv[m, 2 * PG : 3 * PG, :]
            flags = jnp.where(row == m, grecv[m, 3 * PG :, :].astype(f32), flags)
        qb[za, BLOCK:, :] = flags.astype(bf16)
        kb[y, BLOCK:, :] = flags.astype(bf16)
        for copy in scores_copies() + values_copies():
            copy.start()

    def keyframe_attention():
        for copy in scores_copies():
            copy.wait_recv()
        first = lax.broadcasted_iota(jnp.int32, (PG, HD), 1) == 0
        for s in range(4):
            rows = slice(s * BLOCK, (s + 1) * BLOCK)
            qcat[rows, :HD] = qb[s, :BLOCK, :]
            kcat[rows, :HD] = kb[s, :BLOCK, :]
            q_flags = qb[s, BLOCK:, :].astype(f32)
            k_flags = kb[s, BLOCK:, :].astype(f32)
            for m in range(HEADS):
                part = slice(s * BLOCK + m * PG, s * BLOCK + (m + 1) * PG)
                q_flag = jnp.broadcast_to(q_flags[m : m + 1, :], (PG, HD))
                k_flag = jnp.broadcast_to(k_flags[m : m + 1, :], (PG, HD))
                qcat[part, HD:] = jnp.where(first, q_flag, 0.0).astype(bf16)
                kcat[part, HD:] = jnp.where(first, (k_flag - 1.0) * -LOW, 0.0).astype(bf16)
        peaks = {}
        for d in (2, 1, 3, 0):
            rows = pl.ds(pl.multiple_of((za + d) % 4 * BLOCK, BLOCK), BLOCK)
            scores = lax.dot_general(
                qcat[rows, :], kcat[...], (((1,), (1,)), ((), ())), preferred_element_type=f32
            )
            peaks[d] = jnp.max(scores, axis=1, keepdims=True)
            wcat[d] = jnp.exp2((scores - peaks[d]) * LOG2).astype(bf16)
        for copy in values_copies():
            copy.wait_recv()
        for d in (2, 1, 3, 0):
            summed = jnp.dot(wcat[d], vcat[...], preferred_element_type=f32)
            total = summed[:, HD:]
            mean = (summed[:, :HD] / total).astype(bf16)
            tile = split_rows(peaks[d] * LOG2 + jnp.log2(total))
            if d == 0:
                precv[za, :BLOCK, :] = mean
                precv[za, BLOCK:, :] = tile
            else:
                psend[d, :BLOCK, :] = mean
                psend[d, BLOCK:, :] = tile
                partial_copy(d, along_z[d - 1][1]).start()

    def combine_partials():
        for d, p in along_z:
            partial_copy(d, p).wait_recv()
        for block in range(BLOCK // HD):
            rows = slice(block * HD, (block + 1) * HD)
            logs = []
            for s in range(4):
                tile = precv[s, BLOCK:, :].astype(f32)
                logs.append(spread([tile[2 * part + block : 2 * part + block + 1, :] for part in range(3)]))
            peak = jnp.maximum(jnp.maximum(logs[0], logs[1]), jnp.maximum(logs[2], logs[3]))
            total = jnp.zeros((HD, HD), f32)
            summed = jnp.zeros((HD, HD), f32)
            for s in range(4):
                share = jnp.exp2(logs[s] - peak)
                total = total + share
                summed = summed + share * precv[s, rows, :].astype(f32)
            attended = (summed / total).astype(bf16)
            for m in range(HD // PG):
                asend[block * (HD // PG) + m] = attended[m * PG : (m + 1) * PG, :]
        for copy in attended_copies():
            copy.start()
        own_slot.start()
        wo_across().wait_recv()
        wo_beside().start()

    valid = jnp.where(t == 127, ROWS + PL, ROWS + 2 * PL) - FULL

    def local_scores(h, start, rows):
        q = (qv[h, start : start + rows, :].astype(f32) * LOG2).astype(bf16)
        scores = lax.dot_general(q, kf[...], (((1,), (1,)), ((), ())), preferred_element_type=f32)
        last = scores[:, FULL:]
        lane = lax.broadcasted_iota(jnp.int32, last.shape, 1)
        return jnp.concatenate([scores[:, :FULL], jnp.where(lane < valid, last, LOW)], axis=1)

    def local_head(h, unused):
        pl.when(h == 4)(keyframe_attention)
        pl.when(h == 7)(combine_partials)
        for copy in head_copies(h):
            copy.wait()
        for copy in anchor_copies(h):
            copy.wait_recv()
        pad = jnp.zeros((KEYS - ROWS - 2 * PL, HD), f32)
        kf[...] = jnp.concatenate([x[h].astype(f32) for x in (kv, akv, nkv)] + [pad], axis=0).astype(bf16)
        va[:, :HD] = jnp.concatenate([x[h].astype(f32) for x in (vv, avv, nvv)] + [pad], axis=0).astype(bf16)
        starts = [sum(CHUNKS[:i]) for i in range(len(CHUNKS))]
        scores = local_scores(h, starts[0], CHUNKS[0])
        for i, (start, rows) in enumerate(zip(starts, CHUNKS)):
            now = scores
            if i + 1 < len(CHUNKS):
                scores = local_scores(h, starts[i + 1], CHUNKS[i + 1])
            peak = jnp.max(now, axis=1, keepdims=True)
            weights = jnp.exp2((now - peak).astype(bf16))
            summed = jnp.dot(weights, va[...], preferred_element_type=f32)
            ov[h, start : start + rows, :] = (summed[:, :HD] / summed[:, HD:]).astype(bf16)
        out_copy(h).start()
        return unused

    gather_blocks()
    lax.fori_loop(0, HEADS, local_head, 0)

    def finish(h, unused):
        out_copy(h).wait()
        for copy in anchor_copies(h):
            copy.wait_send()
        return unused

    lax.fori_loop(0, HEADS, finish, 0)
    for copy in member_copies() + scores_copies() + values_copies() + [partial_copy(d, p) for d, p in along_z]:
        copy.wait_send()
    for copy in attended_copies() + [wo_beside()]:
        copy.wait()
    wo_across().wait_send()
    own_slot.wait()
    wo_copy.wait()


def project_kernel(att, wo_mine, wo_other, rows, gout, lout, out_sem):
    mp = lax.axis_index("mp")
    move = pltpu.make_async_copy(rows, lout, out_sem)
    move.start()
    total = jnp.zeros(gout.shape, f32)
    for side, wo in ((mp, wo_mine), (1 - mp, wo_other)):
        attended = jnp.concatenate([att[side * HEADS + h] for h in range(HEADS)], axis=1)
        total = total + jnp.dot(attended, wo[...], preferred_element_type=f32)
    gout[...] = total.astype(bf16)
    move.wait()


def body(*args):
    dma = pltpu.SemaphoreType.DMA
    vmem = lambda *shape: pltpu.VMEM(shape, bf16)
    anywhere = pl.BlockSpec(memory_space=pl.ANY)
    in_vmem = pl.BlockSpec(memory_space=pltpu.VMEM)
    width = HEADS * HD
    att, wo_other, wo_mine, rows = pl.pallas_call(
        kernel,
        name="keyframe_and_infill",
        out_shape=(vmem(2 * HEADS, PG, HD), vmem(width, width), vmem(width, width), vmem(ROWS, width)),
        in_specs=[anywhere] * 3 + [pl.BlockSpec(memory_space=pltpu.SMEM)] + [anywhere] * 6,
        out_specs=(anywhere,) * 4,
        scratch_shapes=[
            vmem(PG, width), vmem(PG, width), vmem(PG, width),
            vmem(HEADS, 3 * PG + FLAG, HD), vmem(HEADS, 3 * PG + FLAG, HD),
            vmem(4, BLOCK + FLAG, HD), vmem(4, BLOCK + FLAG, HD),
            vmem(4 * BLOCK, 2 * HD), vmem(4 * BLOCK, 2 * HD), vmem(4 * BLOCK, 2 * HD), vmem(4, BLOCK, 4 * BLOCK),
            vmem(4, BLOCK + FLAG, HD), vmem(4, BLOCK + FLAG, HD), vmem(HEADS, PG, HD),
            vmem(HEADS, ROWS, HD), vmem(HEADS, ROWS, HD), vmem(HEADS, ROWS, HD),
            vmem(HEADS, PL, HD), vmem(HEADS, PL, HD), vmem(HEADS, PL, HD), vmem(HEADS, PL, HD),
            vmem(HEADS, ROWS, HD), vmem(KEYS, HD), vmem(KEYS, 2 * HD),
            dma((6,)), dma((5, HEADS)), dma((HEADS,)),
            dma((8,)), dma((8,)), dma((4,)), dma((4,)), dma((4,)), dma((4,)), dma((4,)), dma((4,)), dma((4,)), dma((4,)),
            dma((16,)), dma((16,)), dma((2,)), dma((2,)), dma((2, HEADS)), dma((2, HEADS)),
        ],
        compiler_params=pltpu.CompilerParams(
            collective_id=1, has_side_effects=True, vmem_limit_bytes=44 * 2**20
        ),
    )(*[arg if arg.ndim == 1 else pltpu.with_memory_space_constraint(arg, pltpu.HBM) for arg in args])
    return pl.pallas_call(
        project_kernel,
        name="projection",
        out_shape=(
            jax.ShapeDtypeStruct((PG, width), bf16),
            jax.ShapeDtypeStruct((ROWS, width), bf16),
        ),
        in_specs=[in_vmem] * 3 + [anywhere],
        out_specs=(in_vmem, anywhere),
        scratch_shapes=[dma],
        compiler_params=pltpu.CompilerParams(vmem_limit_bytes=8 * 2**20),
    )(att, wo_mine, wo_other, rows)


def solution(mesh):
    whole, rows = P("tm", "mp"), P("mp", None)
    return jax.shard_map(
        body,
        mesh=mesh,
        in_specs=(whole, whole, whole, P("tm"), rows) + (whole,) * 5,
        out_specs=(whole, whole),
        check_vma=False,
    )
```

```python
import math

import jax
import jax.numpy as jnp
from jax import lax
from jax.experimental import pallas as pl
from jax.experimental.pallas import tpu as pltpu
from jax.sharding import PartitionSpec as P

HD = 128
HEADS = 8
PG = 32
PL = 88
ROWS = 968
KEYS = 1152
FULL = 1024
CHUNKS = (240, 240, 240, 248)
FLAG = 16
BLOCK = PG * HEADS
MESH = pl.DeviceIdType.MESH
LOG2 = math.log2(math.e) / math.sqrt(HD)
LOW = -1e30
bf16, f32 = jnp.bfloat16, jnp.float32


def spread(parts):
    shape = (HD, HD)
    diagonal = lax.broadcasted_iota(jnp.int32, shape, 0) == lax.broadcasted_iota(jnp.int32, shape, 1)
    wide = [jnp.where(diagonal, jnp.broadcast_to(part, shape), 0.0).astype(bf16) for part in parts]
    ones = jnp.ones((len(parts) * HD, HD), bf16)
    return jnp.dot(jnp.concatenate(wide, axis=1), ones, preferred_element_type=f32)


def split_rows(wide):
    shape = (HD, HD)
    diagonal = lax.broadcasted_iota(jnp.int32, shape, 0) == lax.broadcasted_iota(jnp.int32, shape, 1)
    row = lax.broadcasted_iota(jnp.int32, (FLAG, HD), 0)
    tile = jnp.zeros((FLAG, HD), f32)
    blocks = wide.shape[0] // HD
    for block in range(blocks):
        rest = jnp.sum(jnp.where(diagonal, wide[block * HD : (block + 1) * HD], 0.0), axis=0, keepdims=True)
        for part in range(3):
            piece = rest.astype(bf16).astype(f32)
            tile = jnp.where(row == part * blocks + block, jnp.broadcast_to(piece, tile.shape), tile)
            rest = rest - piece
    return tile.astype(bf16)


def kernel(
    gq, gk, gv, mask, wo, lq, lk, lv, ak, av, att, wo_other, wo_mine, lout,
    gq_v, gk_v, gv_v, gsrc, grecv, qb, kb, qcat, kcat, vcat, psend, precv, asend, qv, kv, vv, akv, avv, nkv, nvv, ov, kf, va,
    in_sem, head_sem, out_sem, a_send, a_recv, q_send, q_recv, k_send, k_recv, v_send, v_recv, p_send, p_recv,
    o_send, o_recv, w_send, w_recv, n_send, n_recv,
):
    t, mp = lax.axis_index("tm"), lax.axis_index("mp")
    y, xl, za, zb, c = t // 32, (t // 16) % 2, (t // 4) % 4, (t // 2) % 2, t % 2
    g = xl * 4 + zb * 2 + c

    def place(y, xl, za, zb, c):
        return y * 32 + xl * 16 + za * 4 + zb * 2 + c

    group = []
    for rel in range(8):
        x2, z2, c2 = (xl + rel // 4) % 2, (zb + rel // 2 % 2) % 2, (c + rel % 2) % 2
        group.append((rel, x2 * 4 + z2 * 2 + c2, place(y, x2, za, z2, c2)))
    members = group[1:]
    across = place(y, 1 - xl, za, zb, c)
    sibling = place(y, xl, za, zb, 1 - c)
    along_z = [(d, place(y, xl, (za + d) % 4, zb, c)) for d in (1, 2, 3)]
    along_y = [(d, place((y + d) % 4, xl, za, zb, c)) for d in (1, 2, 3)]
    before = (t + 127) % 128
    other = (t + 127 + 2 * c) % 128

    own = [
        pltpu.make_async_copy(src, dst, in_sem.at[i])
        for i, (src, dst) in enumerate(((gq, gq_v), (gk, gk_v), (gv, gv_v)))
    ]
    for copy in own:
        copy.start()

    barrier = pltpu.get_barrier_semaphore()
    partners = [(along_z[d][1], mp) for d in (1, 0, 2)] + [(along_y[d][1], mp) for d in (1, 0, 2)]
    partners += [(m[2], mp) for m in members[::-1]] + [(other, mp)] + [(m[2], 1 - mp) for m in group]
    for partner, side in partners:
        pl.semaphore_signal(barrier, inc=1, device_id={"tm": partner, "mp": side}, device_id_type=MESH)

    def remote(src, dst, send, recv, partner, side=mp):
        return pltpu.make_async_remote_copy(
            src_ref=src, dst_ref=dst, send_sem=send, recv_sem=recv,
            device_id={"tm": partner, "mp": side}, device_id_type=MESH,
        )

    def head_columns(h):
        return pl.ds(h * HD, HD)

    def head_copies(h):
        pairs = ((lq, qv), (lk, kv), (lv, vv), (ak, akv), (av, avv))
        return [
            pltpu.make_async_copy(src.at[:, head_columns(h)], dst.at[h], head_sem.at[i, h])
            for i, (src, dst) in enumerate(pairs)
        ]

    def out_copy(h):
        return pltpu.make_async_copy(ov.at[h], lout.at[:, head_columns(h)], out_sem.at[h])

    def anchor_copies(h):
        return [
            remote(src.at[:, head_columns(h)], dst.at[h], n_send.at[i, h], n_recv.at[i, h], before)
            for i, (src, dst) in enumerate(((ak, nkv), (av, nvv)))
        ]

    def member_copies():
        return [remote(gsrc.at[m], grecv.at[g], a_send.at[rel], a_recv.at[rel], p) for rel, m, p in members]

    def scores_copies():
        return [remote(qb.at[za], qb.at[za], q_send.at[d], q_recv.at[d], along_z[d - 1][1]) for d in (2, 1, 3)] + [
            remote(kb.at[y], kb.at[y], k_send.at[d], k_recv.at[d], along_y[d - 1][1]) for d in (2, 1, 3)
        ]

    def values_copies():
        rows = vcat.at[pl.ds(pl.multiple_of(y * BLOCK, BLOCK), BLOCK), :HD]
        return [remote(rows, rows, v_send.at[d], v_recv.at[d], along_y[d - 1][1]) for d in (2, 1, 3)]

    def partial_copy(d, p):
        return remote(psend.at[d], precv.at[za], p_send.at[d], p_recv.at[d], p)

    def attended_copies():
        slot = att.at[mp * HEADS + g]
        return [
            remote(asend.at[m], slot, o_send.at[rel + 8 * i], o_recv.at[rel + 8 * i], p, side)
            for i, side in ((1, 1 - mp), (0, mp))
            for rel, m, p in members[::-1] + group[:i]
        ]

    half = HEADS * HD
    own_half = pl.ds(pl.multiple_of(c * (half // 2), half // 2), half // 2)

    def wo_across():
        src = wo.at[own_half, pl.ds(pl.multiple_of((1 - mp) * half, half), half)]
        return remote(src, wo_other.at[own_half, :], w_send.at[0], w_recv.at[0], across, 1 - mp)

    def wo_beside():
        rows = wo_other.at[own_half, :]
        return remote(rows, rows, w_send.at[1], w_recv.at[1], sibling)

    mine = pl.ds(pl.multiple_of(mp * half, half), half)
    wo_copy = pltpu.make_async_copy(wo.at[:, mine], wo_mine, in_sem.at[5])
    own_slot = pltpu.make_async_copy(asend.at[g], att.at[mp * HEADS + g], in_sem.at[4])

    for copy in own:
        copy.wait()
    given = jnp.full((FLAG, HD), mask[0].astype(f32), f32).astype(bf16)
    for h in range(HEADS):
        columns = slice(h * HD, (h + 1) * HD)
        gsrc[h, :PG, :] = gq_v[:, columns]
        gsrc[h, PG : 2 * PG, :] = gk_v[:, columns]
        gsrc[h, 2 * PG : 3 * PG, :] = gv_v[:, columns]
        gsrc[h, 3 * PG :, :] = given
    pl.semaphore_wait(barrier, len(partners))
    for copy in member_copies()[::-1]:
        copy.start()

    def start_head(h, unused):
        for copy in anchor_copies(h) + head_copies(h):
            copy.start()
        return unused

    lax.fori_loop(0, HEADS, start_head, 0)
    wo_across().start()
    wo_copy.start()
    grecv[g] = gsrc[g]
    va[:, HD:] = jnp.ones((KEYS, HD), bf16)
    vcat[:, HD:] = jnp.ones((4 * BLOCK, HD), bf16)

    def gather_blocks():
        for copy in member_copies():
            copy.wait_recv()
        row = lax.broadcasted_iota(jnp.int32, (FLAG, HD), 0)
        flags = jnp.zeros((FLAG, HD), f32)
        for m in range(HEADS):
            rows = slice(m * PG, (m + 1) * PG)
            qb[za, rows, :] = grecv[m, :PG, :]
            kb[y, rows, :] = grecv[m, PG : 2 * PG, :]
            vcat[pl.ds(pl.multiple_of(y * BLOCK + m * PG, PG), PG), :HD] = grecv[m, 2 * PG : 3 * PG, :]
            flags = jnp.where(row == m, grecv[m, 3 * PG :, :].astype(f32), flags)
        qb[za, BLOCK:, :] = flags.astype(bf16)
        kb[y, BLOCK:, :] = flags.astype(bf16)
        for copy in scores_copies() + values_copies():
            copy.start()

    def keyframe_attention():
        for copy in scores_copies():
            copy.wait_recv()
        first = lax.broadcasted_iota(jnp.int32, (PG, HD), 1) == 0
        for s in range(4):
            rows = slice(s * BLOCK, (s + 1) * BLOCK)
            qcat[rows, :HD] = qb[s, :BLOCK, :]
            kcat[rows, :HD] = kb[s, :BLOCK, :]
            q_flags = qb[s, BLOCK:, :].astype(f32)
            k_flags = kb[s, BLOCK:, :].astype(f32)
            for m in range(HEADS):
                part = slice(s * BLOCK + m * PG, s * BLOCK + (m + 1) * PG)
                q_flag = jnp.broadcast_to(q_flags[m : m + 1, :], (PG, HD))
                k_flag = jnp.broadcast_to(k_flags[m : m + 1, :], (PG, HD))
                qcat[part, HD:] = jnp.where(first, q_flag, 0.0).astype(bf16)
                kcat[part, HD:] = jnp.where(first, (k_flag - 1.0) * -LOW, 0.0).astype(bf16)
        for copy in values_copies():
            copy.wait_recv()
        for d in (2, 1, 3, 0):
            rows = pl.ds(pl.multiple_of((za + d) % 4 * BLOCK, BLOCK), BLOCK)
            scores = lax.dot_general(
                qcat[rows, :], kcat[...], (((1,), (1,)), ((), ())), preferred_element_type=f32
            )
            peak = jnp.max(scores, axis=1, keepdims=True)
            weights = jnp.exp2((scores - peak) * LOG2).astype(bf16)
            summed = jnp.dot(weights, vcat[...], preferred_element_type=f32)
            total = summed[:, HD:]
            mean = (summed[:, :HD] / total).astype(bf16)
            tile = split_rows(peak * LOG2 + jnp.log2(total))
            if d == 0:
                precv[za, :BLOCK, :] = mean
                precv[za, BLOCK:, :] = tile
            else:
                psend[d, :BLOCK, :] = mean
                psend[d, BLOCK:, :] = tile
                partial_copy(d, along_z[d - 1][1]).start()

    def combine_partials():
        for d, p in along_z:
            partial_copy(d, p).wait_recv()
        for block in range(BLOCK // HD):
            rows = slice(block * HD, (block + 1) * HD)
            logs = []
            for s in range(4):
                tile = precv[s, BLOCK:, :].astype(f32)
                logs.append(spread([tile[2 * part + block : 2 * part + block + 1, :] for part in range(3)]))
            peak = jnp.maximum(jnp.maximum(logs[0], logs[1]), jnp.maximum(logs[2], logs[3]))
            total = jnp.zeros((HD, HD), f32)
            summed = jnp.zeros((HD, HD), f32)
            for s in range(4):
                share = jnp.exp2(logs[s] - peak)
                total = total + share
                summed = summed + share * precv[s, rows, :].astype(f32)
            attended = (summed / total).astype(bf16)
            for m in range(HD // PG):
                asend[block * (HD // PG) + m] = attended[m * PG : (m + 1) * PG, :]
        for copy in attended_copies():
            copy.start()
        own_slot.start()
        wo_across().wait_recv()
        wo_beside().start()

    valid = jnp.where(t == 127, ROWS + PL, ROWS + 2 * PL) - FULL

    def local_scores(h, start, rows):
        q = (qv[h, start : start + rows, :].astype(f32) * LOG2).astype(bf16)
        scores = lax.dot_general(q, kf[...], (((1,), (1,)), ((), ())), preferred_element_type=f32)
        last = scores[:, FULL:]
        lane = lax.broadcasted_iota(jnp.int32, last.shape, 1)
        return jnp.concatenate([scores[:, :FULL], jnp.where(lane < valid, last, LOW)], axis=1)

    def local_head(h, unused):
        pl.when(h == 4)(keyframe_attention)
        pl.when(h == 7)(combine_partials)
        for copy in head_copies(h):
            copy.wait()
        for copy in anchor_copies(h):
            copy.wait_recv()
        pad = jnp.zeros((KEYS - ROWS - 2 * PL, HD), f32)
        kf[...] = jnp.concatenate([x[h].astype(f32) for x in (kv, akv, nkv)] + [pad], axis=0).astype(bf16)
        va[:, :HD] = jnp.concatenate([x[h].astype(f32) for x in (vv, avv, nvv)] + [pad], axis=0).astype(bf16)
        starts = [sum(CHUNKS[:i]) for i in range(len(CHUNKS))]
        scores = local_scores(h, starts[0], CHUNKS[0])
        for i, (start, rows) in enumerate(zip(starts, CHUNKS)):
            now = scores
            if i + 1 < len(CHUNKS):
                scores = local_scores(h, starts[i + 1], CHUNKS[i + 1])
            peak = jnp.max(now, axis=1, keepdims=True)
            weights = jnp.exp2((now - peak).astype(bf16))
            summed = jnp.dot(weights, va[...], preferred_element_type=f32)
            ov[h, start : start + rows, :] = (summed[:, :HD] / summed[:, HD:]).astype(bf16)
        out_copy(h).start()
        return unused

    gather_blocks()
    lax.fori_loop(0, HEADS, local_head, 0)

    def finish(h, unused):
        out_copy(h).wait()
        for copy in anchor_copies(h):
            copy.wait_send()
        return unused

    lax.fori_loop(0, HEADS, finish, 0)
    for copy in member_copies() + scores_copies() + values_copies() + [partial_copy(d, p) for d, p in along_z]:
        copy.wait_send()
    for copy in attended_copies() + [wo_beside()]:
        copy.wait()
    wo_across().wait_send()
    own_slot.wait()
    wo_copy.wait()


def project_kernel(att, wo_mine, wo_other, rows, gout, lout, out_sem):
    mp = lax.axis_index("mp")
    move = pltpu.make_async_copy(rows, lout, out_sem)
    move.start()
    total = jnp.zeros(gout.shape, f32)
    for side, wo in ((mp, wo_mine), (1 - mp, wo_other)):
        attended = jnp.concatenate([att[side * HEADS + h] for h in range(HEADS)], axis=1)
        total = total + jnp.dot(attended, wo[...], preferred_element_type=f32)
    gout[...] = total.astype(bf16)
    move.wait()


def body(*args):
    dma = pltpu.SemaphoreType.DMA
    vmem = lambda *shape: pltpu.VMEM(shape, bf16)
    anywhere = pl.BlockSpec(memory_space=pl.ANY)
    in_vmem = pl.BlockSpec(memory_space=pltpu.VMEM)
    width = HEADS * HD
    att, wo_other, wo_mine, rows = pl.pallas_call(
        kernel,
        name="keyframe_and_infill",
        out_shape=(vmem(2 * HEADS, PG, HD), vmem(width, width), vmem(width, width), vmem(ROWS, width)),
        in_specs=[anywhere] * 3 + [pl.BlockSpec(memory_space=pltpu.SMEM)] + [anywhere] * 6,
        out_specs=(anywhere,) * 4,
        scratch_shapes=[
            vmem(PG, width), vmem(PG, width), vmem(PG, width),
            vmem(HEADS, 3 * PG + FLAG, HD), vmem(HEADS, 3 * PG + FLAG, HD),
            vmem(4, BLOCK + FLAG, HD), vmem(4, BLOCK + FLAG, HD),
            vmem(4 * BLOCK, 2 * HD), vmem(4 * BLOCK, 2 * HD), vmem(4 * BLOCK, 2 * HD),
            vmem(4, BLOCK + FLAG, HD), vmem(4, BLOCK + FLAG, HD), vmem(HEADS, PG, HD),
            vmem(HEADS, ROWS, HD), vmem(HEADS, ROWS, HD), vmem(HEADS, ROWS, HD),
            vmem(HEADS, PL, HD), vmem(HEADS, PL, HD), vmem(HEADS, PL, HD), vmem(HEADS, PL, HD),
            vmem(HEADS, ROWS, HD), vmem(KEYS, HD), vmem(KEYS, 2 * HD),
            dma((6,)), dma((5, HEADS)), dma((HEADS,)),
            dma((8,)), dma((8,)), dma((4,)), dma((4,)), dma((4,)), dma((4,)), dma((4,)), dma((4,)), dma((4,)), dma((4,)),
            dma((16,)), dma((16,)), dma((2,)), dma((2,)), dma((2, HEADS)), dma((2, HEADS)),
        ],
        compiler_params=pltpu.CompilerParams(
            collective_id=1, has_side_effects=True, vmem_limit_bytes=44 * 2**20
        ),
    )(*[arg if arg.ndim == 1 else pltpu.with_memory_space_constraint(arg, pltpu.HBM) for arg in args])
    return pl.pallas_call(
        project_kernel,
        name="projection",
        out_shape=(
            jax.ShapeDtypeStruct((PG, width), bf16),
            jax.ShapeDtypeStruct((ROWS, width), bf16),
        ),
        in_specs=[in_vmem] * 3 + [anywhere],
        out_specs=(in_vmem, anywhere),
        scratch_shapes=[dma],
        compiler_params=pltpu.CompilerParams(vmem_limit_bytes=8 * 2**20),
    )(att, wo_mine, wo_other, rows)


def solution(mesh):
    whole, rows = P("tm", "mp"), P("mp", None)
    return jax.shard_map(
        body,
        mesh=mesh,
        in_specs=(whole, whole, whole, P("tm"), rows) + (whole,) * 5,
        out_specs=(whole, whole),
        check_vma=False,
    )
```
